32 devices in a mesh: lat: 4 (over z), lon: 8 (over y, x, core).
Axes of the slice: x: 2, y: 2, z: 4, core: 2. Of those that a mesh axis runs over, the one named last changes fastest.
Arguments:
- u_wind: float32 [1440, 16, 128], P('lon', 'lat'), may hold values from -6 to 6
- v_wind: float32 [1440, 16, 128], P('lon', 'lat'), may hold values from -6 to 6
- height: float32 [1440, 16, 128], P('lon', 'lat'), may hold values from -6 to 6
- wave_speed: float32 [128], replicated, may hold values from 0.1 to 0.4
- cutoff: int32 [16], replicated, may hold values from 1 to 720, as said below
Outputs:
- u_next: float32 [1440, 16, 128], P('lon', 'lat')
- v_next: float32 [1440, 16, 128], P('lon', 'lat')
- h_next: float32 [1440, 16, 128], P('lon', 'lat')
The draws below stay inside these ranges and needn't reach their ends.
Inputs may be any that keep to these rules, and one draw needn't show every extreme that they name: `cutoff`: rows 4 to 11, within 45 degrees of the equator, hold 720, which keeps every wavenumber; the other rows hold smaller values, 1 on the two outermost rows.
All inputs are finite; a program needn't handle non-finite values.
Results may differ from the reference program's by a relative error of at most 0.00005.
Values sent between devices are 32-bit elements; how exact they have to be, the bound alone decides.
A program may use at most 64 MiB of HBM per device.

```python
import math
import jax
import jax.numpy as jnp

NLON = 1440
LEV = 128
NLAT = 16


def draw_cutoff(key, part):
    row_ids = jnp.arange(NLAT, dtype=jnp.int32)
    pole_dist = jnp.minimum(row_ids, NLAT - 1 - row_ids)
    quarter = NLAT // 4
    half_modes = NLON // 2
    base_cut = 1 + pole_dist * (half_modes - 1) // quarter
    jitter = jax.random.randint(key, (NLAT,), 0, 1 + half_modes // 16, dtype=jnp.int32)
    jitter = jitter * (pole_dist > 0).astype(jnp.int32)
    polar_cut = jnp.minimum(base_cut + jitter, half_modes)
    return jnp.where(pole_dist >= quarter, half_modes, polar_cut).astype(jnp.int32)


def level_of(own_key, extent, shards, smallest, top_value):
    level, own = 1.0, jax.random.fold_in(own_key, 6)
    for position, blocks in shards:
        steps = jnp.exp(jax.random.uniform(jax.random.fold_in(own, position), (blocks,), jnp.float32, smallest / len(shards), top_value / len(shards)))
        level = level * jnp.repeat(steps, extent[position] // blocks).reshape([-1 if axis == position else 1 for axis in range(len(extent))])
    return level


def bell_draw(key, extent, deviation, limit, shards=(), held_as=jnp.bfloat16):
    loudness = level_of(key, extent, shards, -0.22, 0.18) if shards else 1.0
    entries = jax.random.normal(key, extent, jnp.float32) * deviation * loudness
    return jnp.minimum(jnp.maximum(entries, -limit), limit).astype(held_as)


def setup_inputs(seed: int = 0) -> dict:
    seeds = jax.random.split(jax.random.key(seed), 6)
    return {
        "u_wind": bell_draw(seeds[0], (NLON, NLAT, LEV), 1.0, 6.0, ((0, 8), (1, 4)), jnp.float32),
        "v_wind": bell_draw(seeds[1], (NLON, NLAT, LEV), 1.0, 6.0, ((0, 8), (1, 4)), jnp.float32),
        "height": bell_draw(seeds[2], (NLON, NLAT, LEV), 1.0, 6.0, ((0, 8), (1, 4)), jnp.float32),
        "wave_speed": jnp.clip(jnp.exp(jax.random.uniform(seeds[3], (LEV,), jnp.float32, math.log(0.1), math.log(0.4))), 0.1, 0.4),
        "cutoff": draw_cutoff(jax.random.fold_in(seeds[5], 71), 0),
    }


coriolis_rate = 0.25


def reference(u_wind, v_wind, height, wave_speed, cutoff):
    row_ids = jnp.arange(NLAT, dtype=jnp.int32)
    latitude = 0.5 * math.pi - (row_ids.astype(jnp.float32) + 0.5) * (math.pi / NLAT)
    cos_lat = jnp.cos(latitude)[:, None]
    sin_lat = jnp.sin(latitude)[:, None]
    stretch = (NLON / (2.0 * NLAT)) / cos_lat
    speed_col = wave_speed[None, None, :]
    wavenum = jnp.arange(NLON // 2 + 1, dtype=jnp.int32)
    keep_mask = (wavenum[:, None] <= cutoff[None, :])[:, :, None]

    def smooth(field):
        spectrum = jnp.fft.rfft(field, axis=0)
        spectrum = jnp.where(keep_mask, spectrum, 0.0)
        return jnp.fft.irfft(spectrum, n=NLON, axis=0).astype(jnp.float32)

    def zonal(field):
        return (jnp.roll(field, -1, 0) - jnp.roll(field, 1, 0)) * 0.5

    def merid(field):
        padded = jnp.pad(field, ((0, 0), (1, 1), (0, 0)))
        return (padded[:, :-2, :] - padded[:, 2:, :]) * 0.5

    def tendency(u_now, v_now, h_now):
        zonal_u = zonal(u_now)
        zonal_h = zonal(h_now)
        merid_vc = merid(v_now * cos_lat)
        merid_h = merid(h_now)
        tend_u = coriolis_rate * sin_lat * v_now - speed_col * (stretch * zonal_h)
        tend_v = -coriolis_rate * sin_lat * u_now - speed_col * merid_h
        tend_h = -speed_col * (stretch * zonal_u + merid_vc / cos_lat)
        return (smooth(tend_u), smooth(tend_v), smooth(tend_h))

    fields = (u_wind, v_wind, height)
    change = tendency(u_wind, v_wind, height)
    first = [fields[n] + change[n] for n in range(3)]
    change = tendency(first[0], first[1], first[2])
    second = [0.75 * fields[n] + 0.25 * (first[n] + change[n]) for n in range(3)]
    change = tendency(second[0], second[1], second[2])
    third = [(1.0 / 3.0) * fields[n] + (2.0 / 3.0) * (second[n] + change[n]) for n in range(3)]
    return (third[0], third[1], third[2])
```

```python
import functools
import math

import jax
import jax.numpy as jnp
import numpy as np
from jax import lax
from jax.experimental import pallas as pl
from jax.experimental.pallas import tpu as pltpu
from jax.sharding import PartitionSpec as P

coriolis_rate = 0.25
MESH = pl.DeviceIdType.MESH
RADIX = 8
ROOT = math.sqrt(0.5)


def round_up(value, unit):
    return -(-value // unit) * unit


def widened(table):
    hi = table.astype(jnp.bfloat16)
    lo = (table - hi.astype(np.float64)).astype(jnp.bfloat16)
    return np.concatenate([hi, hi, lo], axis=-1)


def tables(points, cells, pad_cells):
    part = points // RADIX
    subs = part // cells
    pad = subs * pad_cells
    place = np.concatenate([np.arange(cells) + j * pad_cells for j in range(subs)])
    spots = np.arange(part)
    unit = 2.0 * np.pi / points

    def placed(block):
        out = np.zeros((pad, pad))
        out[: block.shape[0], place] = block
        return out

    half = part // 2
    q = np.arange(half + 1)
    even = (RADIX * q)[:, None] * spots[None, :] % points * unit
    scale = np.where((q == 0) | (q == half), 1.0, 2.0)[:, None]
    first = np.concatenate(
        [np.cos(even) * np.sqrt(scale / points), np.sin(even[1:half]) * np.sqrt(2.0 / points)]
    )
    q = np.arange(half)
    odd = (RADIX * q + RADIX // 2)[:, None] * spots[None, :] % points * unit
    last = np.concatenate([np.cos(odd), np.sin(odd)]) * np.sqrt(2.0 / points)
    real = np.stack([placed(first), placed(last)])
    mixed = []
    for s in (1, 2, 3):
        q = np.arange(part)
        angle = (RADIX * q + s)[:, None] * spots[None, :] % points * unit
        c, d = placed(np.cos(angle)), placed(np.sin(angle))
        mixed.append(np.block([[c, d], [-d, c]]) * np.sqrt(2.0 / points))
    mixed = np.stack(mixed)
    return tuple(
        np.stack([widened(table), widened(np.swapaxes(table, 1, 2))]) for table in (real, mixed)
    )


def geometry(points, bands, rows, width):
    total = rows * bands
    latitude = 0.5 * np.pi - (np.arange(total) + 0.5) * (np.pi / total)
    out = []
    for band in range(bands):
        own = latitude[band * rows : (band + 1) * rows]
        cos_lat, sin_lat = np.repeat(np.cos(own), width), np.repeat(np.sin(own), width)
        stretch = points / (2.0 * total) / cos_lat
        zero, one = np.zeros_like(cos_lat), np.ones_like(cos_lat)
        pairs = (
            (0.5 * stretch, 0.5 * one),
            (0.5 * stretch, zero),
            (0.5 / cos_lat, zero),
            (coriolis_rate * sin_lat, -coriolis_rate * sin_lat),
            (zero, cos_lat),
            (zero, zero),
            (zero, zero),
            (zero, zero),
        )
        out.extend(np.concatenate(pair) for pair in pairs)
    return np.stack(out).astype(np.float32)


def roll(value, shift):
    width = value.shape[-1]
    shift = shift % width
    if shift == 0:
        return value
    if width == 128:
        return pltpu.roll(value, shift, 1)
    return jnp.concatenate([value[:, width - shift :], value[:, : width - shift]], axis=1)


def dot(a, b):
    return jnp.dot(a, b, preferred_element_type=jnp.float32)


def split(value):
    hi = value.astype(jnp.bfloat16)
    return hi, (value - hi.astype(jnp.float32)).astype(jnp.bfloat16)


def kernel(
    dims,
    u_hbm,
    v_hbm,
    h_hbm,
    speed_hbm,
    cutoff_ref,
    geo_hbm,
    real_hbm,
    mixed_hbm,
    u_out,
    v_out,
    h_out,
    u_ref,
    v_ref,
    h_ref,
    speed_ref,
    geo_ref,
    real_t,
    mixed_t,
    send1,
    recv1,
    send2,
    recv2,
    base_uv,
    base_h,
    cur_uv,
    cur_h,
    tend_uv,
    tend_h,
    y_in,
    y_out,
    halo_send,
    halo_recv,
    table_sem,
    send1_sem,
    recv1_sem,
    send2_sem,
    recv2_sem,
    hsend_sem,
    hrecv_sem,
):
    bands, devs, cells, rows, width, pad, wire, half = dims
    points = cells * devs
    part = points // RADIX
    subs = devs // RADIX
    part_pad = subs * pad
    span = rows * width
    slab = 2 * span
    levels = width * devs
    me = lax.axis_index("lon")
    band = lax.axis_index("lat")
    has_north = band > 0
    has_south = band < bands - 1

    local = [
        pltpu.make_async_copy(source, target, table_sem.at[n])
        for n, (source, target) in enumerate(
            (
                (u_hbm, u_ref),
                (v_hbm, v_ref),
                (h_hbm, h_ref),
                (speed_hbm, speed_ref),
                (geo_hbm, geo_ref),
                (real_hbm, real_t),
                (mixed_hbm, mixed_t),
            )
        )
    ]
    for copy in local:
        copy.start()

    barrier = pltpu.get_barrier_semaphore()

    def greet(k, _):
        pl.semaphore_signal(
            barrier, inc=1, device_id={"lon": lax.rem(me + k, devs)}, device_id_type=MESH
        )
        return 0

    lax.fori_loop(1, devs, greet, 0)

    @pl.when(has_north)
    def _():
        pl.semaphore_signal(barrier, inc=1, device_id={"lat": band - 1}, device_id_type=MESH)

    @pl.when(has_south)
    def _():
        pl.semaphore_signal(barrier, inc=1, device_id={"lat": band + 1}, device_id_type=MESH)

    pl.semaphore_wait(
        barrier, devs - 1 + has_north.astype(jnp.int32) + has_south.astype(jnp.int32)
    )

    for copy in local[:3]:
        copy.wait()

    lane_lev = lax.broadcasted_iota(jnp.int32, (cells, levels), 1)
    fields = (u_ref, v_ref, h_ref)
    uv_units = [(fields[n // rows], n % rows, 0) for n in range(2 * rows)]
    h_units = [(h_ref, n % rows, (n // rows) * (cells - half)) for n in range(2 * rows)]

    def packed(units, count, peer):
        total = jnp.zeros((count, levels), jnp.float32)
        lane = lane_lev[:count]
        for n, (ref, row, start) in enumerate(units):
            piece = ref[pl.ds(row + rows * start, count, stride=rows), :]
            shift = lax.rem(n * width - peer * width + levels, levels)
            piece = pltpu.roll(piece, shift, 1)
            total = jnp.where((lane >= n * width) & (lane < (n + 1) * width), piece, total)
        return total[:, :slab]

    def fill(target, slot, peer):
        target[slot, wire - 8 : wire, :] = jnp.zeros((8, slab), jnp.float32)
        target[slot, 0:cells, :] = packed(uv_units, cells, peer)
        target[slot, wire : wire + half, :] = packed(h_units, half, peer)

    def copy1(peer, index):
        return pltpu.make_async_remote_copy(
            src_ref=send1.at[peer],
            dst_ref=recv1.at[index],
            send_sem=send1_sem.at[peer],
            recv_sem=recv1_sem.at[index],
            device_id={"lon": peer},
            device_id_type=MESH,
        )

    def copy2(peer, index):
        return pltpu.make_async_remote_copy(
            src_ref=send2.at[peer],
            dst_ref=recv2.at[index],
            send_sem=send2_sem.at[peer],
            recv_sem=recv2_sem.at[index],
            device_id={"lon": peer},
            device_id_type=MESH,
        )

    def out1(k, _):
        peer = lax.rem(me + k, devs)
        fill(send1, peer, peer)
        copy1(peer, me).start()
        return 0

    lax.fori_loop(1, devs, out1, 0)
    fill(recv1, me, me)

    for copy in local[3:5]:
        copy.wait()
    lane = lax.broadcasted_iota(jnp.int32, (1, slab), 1)
    low = lane < span
    groups = devs // 4
    my_group = me // 4
    all_speeds = jnp.broadcast_to(speed_ref[...], (8, levels))
    own_first = pltpu.roll(all_speeds, lax.rem(levels - me * width, levels), 1)
    lane8 = lax.broadcasted_iota(jnp.int32, (8, levels), 1)
    speed = jnp.zeros((8, levels), jnp.float32)
    cut = jnp.zeros((1, slab), jnp.float32)
    for n in range(2 * rows):
        moved = pltpu.roll(own_first, n * width, 1) if n else own_first
        speed = jnp.where((lane8 >= n * width) & (lane8 < (n + 1) * width), moved, speed)
        row_cut = cutoff_ref[band * rows + n % rows].astype(jnp.float32)
        cut = jnp.where((lane >= n * width) & (lane < (n + 1) * width), row_cut, cut)
    cut = jnp.concatenate([cut, cut], axis=1)
    geo = geo_ref[pl.ds(pl.multiple_of(band * 8, 8), 8), :]
    scaled = geo * speed[:, :slab]
    k1, k2, k3 = scaled[0:1], scaled[1:2], scaled[2:3]
    fcor, cosl = geo[3:4], geo[4:5]

    @pl.when(band == 0)
    def _():
        for t in range(3):
            halo_recv[t, 0] = jnp.zeros(halo_recv.shape[2:], jnp.float32)

    @pl.when(band == bands - 1)
    def _():
        for t in range(3):
            halo_recv[t, 1] = jnp.zeros(halo_recv.shape[2:], jnp.float32)

    def unpack(b):
        uv = recv1[b, 0:wire, :]
        hp = recv1[b, wire : wire + half, :]
        other = roll(hp, span)
        for buf_uv, buf_h, at in ((base_uv, base_h, 0), (cur_uv, cur_h, 8)):
            zeros = jnp.zeros((16, slab), jnp.float32)
            buf_uv[b, at + pad - 16 : at + pad, :] = zeros
            buf_h[b, at + pad - 16 : at + pad, :] = zeros
            if at:
                buf_uv[b, at + pad : at + pad + 8, :] = zeros[:8]
                buf_h[b, at + pad : at + pad + 8, :] = zeros[:8]
            buf_uv[b, at : at + wire, :] = uv
            buf_h[b, at : at + half, :] = hp
            buf_h[b, at + cells - half : at + cells, :] = other

    def halo_copy(t, side, g):
        return pltpu.make_async_remote_copy(
            src_ref=halo_send.at[t, side, g],
            dst_ref=halo_recv.at[t, side, g],
            send_sem=hsend_sem.at[t, side, g],
            recv_sem=hrecv_sem.at[t, side, g],
            device_id={"lat": band + 1 if side == 0 else band - 1},
            device_id_type=MESH,
        )

    def send_halos(t, g):
        south = jnp.zeros((pad, slab), jnp.float32)
        north = jnp.zeros((pad, slab), jnp.float32)
        for j in range(4):
            b = g * 4 + j
            h = cur_h[b, 8 : 8 + pad, :]
            vc = cur_uv[b, 8 : 8 + pad, :] * cosl
            at = 2 * width * j
            on_h = (lane >= at) & (lane < at + width)
            on_v = (lane >= at + width) & (lane < at + 2 * width)
            south = jnp.where(on_h, roll(h, at - (span - width)), south)
            south = jnp.where(on_v, roll(vc, at + width - (slab - width)), south)
            north = jnp.where(on_h, roll(h, at), north)
            north = jnp.where(on_v, roll(vc, at + width - span), north)
        halo_send[t, 0, g] = south
        halo_send[t, 1, g] = north

        @pl.when(has_south)
        def _():
            halo_copy(t, 0, g).start()

        @pl.when(has_north)
        def _():
            halo_copy(t, 1, g).start()

    def in1(k, _):
        g = lax.rem(my_group + k, groups)
        for j in range(4):
            b = g * 4 + j

            @pl.when(b != me)
            def _():
                copy1(b, b).wait_recv()

            unpack(b)
        send_halos(0, g)
        return 0

    lax.fori_loop(0, groups, in1, 0)

    def wrap_rows():
        def one(b, _):
            before = lax.rem(b + devs - 1, devs)
            after = lax.rem(b + 1, devs)
            for buf in (cur_uv, cur_h):
                buf[b, 7:8, :] = buf[before, 7 + cells : 8 + cells, :]
                buf[b, 8 + cells : 9 + cells, :] = buf[after, 8:9, :]
            return 0

        lax.fori_loop(0, devs, one, 0)

    def wait_halos(t, g):
        @pl.when(has_north)
        def _():
            halo_copy(t, 0, g).wait_recv()

        @pl.when(has_south)
        def _():
            halo_copy(t, 1, g).wait_recv()

    def tendencies(t):
        def group(k, _):
            g = lax.rem(my_group + k, groups)
            wait_halos(t, g)
            from_north = halo_recv[t, 0, g]
            from_south = halo_recv[t, 1, g]
            for j in range(4):
                b = g * 4 + j
                at = 2 * width * j
                uv = cur_uv[b, 8 : 8 + pad, :]
                h = cur_h[b, 8 : 8 + pad, :]
                duv = cur_uv[b, 9 : 9 + pad, :] - cur_uv[b, 7 : 7 + pad, :]
                dh = cur_h[b, 9 : 9 + pad, :] - cur_h[b, 7 : 7 + pad, :]
                vc = uv * cosl
                h_n = jnp.where(lane < width, roll(from_north, -at), roll(h, width))
                h_s = jnp.where(
                    lane >= span - width, roll(from_south, span - width - at), roll(h, -width)
                )
                v_n = jnp.where(
                    lane < span + width, roll(from_north, span - width - at), roll(vc, width)
                )
                v_s = jnp.where(
                    lane >= slab - width, roll(from_south, slab - 2 * width - at), roll(vc, -width)
                )
                mh = h_n - h_s
                mv = v_n - v_s
                tend_uv[b] = fcor * roll(uv, span) - k1 * jnp.where(low, dh, roll(mh, span))
                tend_h[b] = -(k2 * duv + k3 * roll(mv, span))
            return 0

        lax.fori_loop(0, groups, group, 0)

    def start_of(s):
        return 3 * part_pad * (s if s < 2 else 2 * s - 2)

    def put(s, half_at, j, piece, value):
        hi, lo = split(value)
        height = part_pad if s < 2 else 2 * part_pad
        at = start_of(s) + half_at * part_pad + j * pad
        columns = slice(piece * slab, (piece + 1) * slab)
        y_in[at : at + pad, columns] = hi
        y_in[at + height : at + height + pad, columns] = lo
        y_in[at + 2 * height : at + 2 * height + pad, columns] = hi

    def forward():
        for j in range(subs):
            for piece, buf in enumerate((tend_uv, tend_h)):
                x = [buf[g * subs + j] for g in range(RADIX)]
                a = [x[n] + x[n + 4] for n in range(4)]
                d = [x[n] - x[n + 4] for n in range(4)]
                plus, minus = a[0] + a[2], a[1] + a[3]
                put(0, 0, j, piece, plus + minus)
                put(1, 0, j, piece, plus - minus)
                less, more = ROOT * (d[1] - d[3]), ROOT * (d[1] + d[3])
                put(2, 0, j, piece, d[0] + less)
                put(2, 1, j, piece, -d[2] - more)
                put(3, 0, j, piece, a[0] - a[2])
                put(3, 1, j, piece, a[3] - a[1])
                put(4, 0, j, piece, d[0] - less)
                put(4, 1, j, piece, d[2] - more)

    def kept(wave, coefs):
        nearest = jnp.minimum(wave, points - wave).astype(jnp.float32)
        hi, lo = split(jnp.where(nearest <= cut, coefs, 0.0))
        return jnp.concatenate([hi, lo, hi], axis=0)

    def through():
        row = lax.broadcasted_iota(jnp.int32, (part_pad, 2 * slab), 0)
        mid = part // 2
        even = RADIX * jnp.where(row <= mid, row, row - mid)
        odd = RADIX * jnp.where(row < mid, row, row - mid) + RADIX // 2
        for s, wave in enumerate((even, odd)):
            at = pl.ds(s * part_pad, part_pad)
            coefs = dot(real_t[0, s], y_in[pl.ds(start_of(s), 3 * part_pad), :])
            y_out[at, :] = dot(real_t[1, s], kept(wave, coefs))
        both = lax.broadcasted_iota(jnp.int32, (2 * part_pad, 2 * slab), 0)
        wave8 = RADIX * jnp.where(both < part_pad, both, both - part_pad)

        for s in range(3):
            at = pl.ds((2 + 2 * s) * part_pad, 2 * part_pad)
            coefs = dot(mixed_t[0, s], y_in[pl.ds(start_of(s + 2), 6 * part_pad), :])
            y_out[at, :] = dot(mixed_t[1, s], kept(wave8 + (s + 1), coefs))

    def backward():
        for j in range(subs):
            for piece, buf in enumerate((tend_uv, tend_h)):
                y = [
                    y_out[pl.ds(n * part_pad + j * pad, pad), piece * slab : (piece + 1) * slab]
                    for n in range(RADIX)
                ]
                plus, minus = y[0] + y[1], y[0] - y[1]
                e, f = y[2] + y[6], y[7] - y[3]
                buf[0 * subs + j] = plus + y[4] + e
                buf[4 * subs + j] = plus + y[4] - e
                buf[2 * subs + j] = plus - y[4] + f
                buf[6 * subs + j] = plus - y[4] - f
                m, n = ROOT * (y[2] - y[6]), ROOT * (y[3] + y[7])
                buf[1 * subs + j] = minus - y[5] + (m - n)
                buf[5 * subs + j] = minus - y[5] - (m - n)
                buf[3 * subs + j] = minus + y[5] - (m + n)
                buf[7 * subs + j] = minus + y[5] + (m + n)

    quarter = rows * bands // 4
    filters = (band * rows < quarter) | (band * rows + rows > rows * bands - quarter)

    for t, (own, new) in enumerate(((0.0, 1.0), (0.75, 0.25), (1.0 / 3.0, 2.0 / 3.0))):
        wrap_rows()
        if t == 0:
            for copy in local[5:]:
                copy.wait()
        tendencies(t)

        @pl.when(filters)
        def _():
            forward()
            through()
            backward()

        def update(k, _):
            g = lax.rem(my_group + k, groups)
            for j in range(4):
                b = g * 4 + j
                for base, cur, tend in ((base_uv, cur_uv, tend_uv), (base_h, cur_h, tend_h)):
                    value = cur[b, 8 : 8 + pad, :] + tend[b]
                    if t > 0:
                        value = own * base[b] + new * value
                    cur[b, 8 : 8 + pad, :] = value
            send_halos(t + 1, g)
            return 0

        if t < 2:
            lax.fori_loop(0, groups, update, 0)

    def result(target, slot, b):
        def final(base, cur, tend, start, count):
            value = cur[b, 8 + start : 8 + start + count, :] + tend[b, start : start + count, :]
            return own * base[b, start : start + count, :] + new * value

        target[slot, 0:wire, :] = final(base_uv, cur_uv, tend_uv, 0, wire)
        h_first = final(base_h, cur_h, tend_h, 0, half)
        h_last = final(base_h, cur_h, tend_h, cells - half, half)
        target[slot, wire : wire + half, :] = jnp.where(low, h_first, roll(h_last, span))

    def out2(k, _):
        peer = lax.rem(me + k, devs)
        result(send2, peer, peer)
        copy2(peer, me).start()
        return 0

    lax.fori_loop(1, devs, out2, 0)
    result(recv2, me, me)

    def in2(k, _):
        peer = lax.rem(me + devs - k, devs)
        copy2(peer, peer).wait_recv()
        return 0

    lax.fori_loop(1, devs, in2, 0)

    def wide(value):
        if slab == levels:
            return value
        fill_up = jnp.zeros((value.shape[0], levels - slab), jnp.float32)
        return jnp.concatenate([value, fill_up], axis=1)

    outs = (u_out, v_out, h_out)

    def gathered(n, first, count):
        total = jnp.zeros((count, levels), jnp.float32)
        here = lane_lev[:count]
        for d in range(devs):
            piece = wide(recv2[d, first : first + count, :])
            piece = pltpu.roll(piece, (d - n) * width % levels, 1)
            total = jnp.where((here >= d * width) & (here < (d + 1) * width), piece, total)
        return total

    for n in range(2 * rows):
        ref = outs[n // rows]
        ref[pl.ds(n % rows, cells, stride=rows), :] = gathered(n, 0, cells)
        start = (n // rows) * (cells - half)
        h_out[pl.ds(n % rows + rows * start, half, stride=rows), :] = gathered(n, wire, half)

    def done(k, _):
        peer = lax.rem(me + k, devs)
        copy1(peer, me).wait_send()
        copy2(peer, me).wait_send()
        return 0

    lax.fori_loop(1, devs, done, 0)

    for t in range(3):
        for g in range(groups):
            @pl.when(has_south)
            def _():
                halo_copy(t, 0, g).wait_send()

            @pl.when(has_north)
            def _():
                halo_copy(t, 1, g).wait_send()


def shards(geo_tab, real_tab, mixed_tab, bands, devs, pad, u_wind, v_wind, height, wave_speed, cutoff):
    cells, rows, levels = u_wind.shape
    width = levels // devs
    slab = 2 * rows * width
    wire = round_up(cells, 8)
    half = round_up(-(-cells // 2), 8)
    f32, bf16 = jnp.float32, jnp.bfloat16
    part_pad = devs // RADIX * pad
    dims = (bands, devs, cells, rows, width, pad, wire, half)
    vmem = pl.BlockSpec(memory_space=pltpu.VMEM)
    anywhere = pl.BlockSpec(memory_space=pl.ANY)
    flat = jax.ShapeDtypeStruct((cells * rows, levels), f32)
    dma = pltpu.SemaphoreType.DMA
    outs = pl.pallas_call(
        functools.partial(kernel, dims),
        out_shape=(flat, flat, flat),
        in_specs=[anywhere] * 4 + [pl.BlockSpec(memory_space=pltpu.SMEM)] + [anywhere] * 3,
        out_specs=(vmem, vmem, vmem),
        scratch_shapes=[
            pltpu.VMEM(flat.shape, f32),
            pltpu.VMEM(flat.shape, f32),
            pltpu.VMEM(flat.shape, f32),
            pltpu.VMEM((1, levels), f32),
            pltpu.VMEM(geo_tab.shape, f32),
            pltpu.VMEM(real_tab.shape, bf16),
            pltpu.VMEM(mixed_tab.shape, bf16),
            pltpu.VMEM((devs, wire + half, slab), f32),
            pltpu.VMEM((devs, wire + half, slab), f32),
            pltpu.VMEM((devs, wire + half, slab), f32),
            pltpu.VMEM((devs, wire + half, slab), f32),
            pltpu.VMEM((devs, pad, slab), f32),
            pltpu.VMEM((devs, pad, slab), f32),
            pltpu.VMEM((devs, pad + 16, slab), f32),
            pltpu.VMEM((devs, pad + 16, slab), f32),
            pltpu.VMEM((devs, pad, slab), f32),
            pltpu.VMEM((devs, pad, slab), f32),
            pltpu.VMEM((3 * RADIX * part_pad, 2 * slab), bf16),
            pltpu.VMEM((RADIX * part_pad, 2 * slab), f32),
            pltpu.VMEM((3, 2, devs // 4, pad, slab), f32),
            pltpu.VMEM((3, 2, devs // 4, pad, slab), f32),
            dma((7,)),
            dma((devs,)),
            dma((devs,)),
            dma((devs,)),
            dma((devs,)),
            dma((3, 2, devs // 4)),
            dma((3, 2, devs // 4)),
        ],
        compiler_params=pltpu.CompilerParams(
            collective_id=0, has_side_effects=True, vmem_limit_bytes=48 * 1024 * 1024
        ),
    )(
        u_wind.reshape(cells * rows, levels),
        v_wind.reshape(cells * rows, levels),
        height.reshape(cells * rows, levels),
        wave_speed.reshape(1, levels),
        cutoff,
        jnp.asarray(geo_tab),
        jnp.asarray(real_tab),
        jnp.asarray(mixed_tab),
    )
    return tuple(out.reshape(cells, rows, levels) for out in outs)


def solution(mesh):
    bands, devs = mesh.shape["lat"], mesh.shape["lon"]

    def step(u_wind, v_wind, height, wave_speed, cutoff):
        points = u_wind.shape[0]
        pad = round_up(points // devs + 1, 16)
        real_tab, mixed_tab = tables(points, points // devs, pad)
        rows, width = u_wind.shape[1] // bands, u_wind.shape[2] // devs
        geo_tab = geometry(points, bands, rows, width)
        spec = P("lon", "lat", None)
        local = functools.partial(shards, geo_tab, real_tab, mixed_tab, bands, devs, pad)
        return jax.shard_map(
            local,
            mesh=mesh,
            in_specs=(spec, spec, spec, P(), P()),
            out_specs=(spec, spec, spec),
            check_vma=False,
        )(u_wind, v_wind, height, wave_speed, cutoff)

    return step
```

```python
import functools
import math

import jax
import jax.numpy as jnp
import numpy as np
from jax import lax
from jax.experimental import pallas as pl
from jax.experimental.pallas import tpu as pltpu
from jax.sharding import PartitionSpec as P

coriolis_rate = 0.25
MESH = pl.DeviceIdType.MESH
RADIX = 8
ROOT = math.sqrt(0.5)


def round_up(value, unit):
    return -(-value // unit) * unit


def widened(table):
    hi = table.astype(jnp.bfloat16)
    lo = (table - hi.astype(np.float64)).astype(jnp.bfloat16)
    return np.concatenate([hi, hi, lo], axis=-1)


def tables(points, cells, pad_cells):
    part = points // RADIX
    subs = part // cells
    pad = subs * pad_cells
    place = np.concatenate([np.arange(cells) + j * pad_cells for j in range(subs)])
    spots = np.arange(part)
    unit = 2.0 * np.pi / points

    def placed(block):
        out = np.zeros((pad, pad))
        out[: block.shape[0], place] = block
        return out

    half = part // 2
    q = np.arange(half + 1)
    even = (RADIX * q)[:, None] * spots[None, :] % points * unit
    scale = np.where((q == 0) | (q == half), 1.0, 2.0)[:, None]
    first = np.concatenate(
        [np.cos(even) * np.sqrt(scale / points), np.sin(even[1:half]) * np.sqrt(2.0 / points)]
    )
    q = np.arange(half)
    odd = (RADIX * q + RADIX // 2)[:, None] * spots[None, :] % points * unit
    last = np.concatenate([np.cos(odd), np.sin(odd)]) * np.sqrt(2.0 / points)
    real = np.stack([placed(first), placed(last)])
    mixed = []
    for s in (1, 2, 3):
        q = np.arange(part)
        angle = (RADIX * q + s)[:, None] * spots[None, :] % points * unit
        c, d = placed(np.cos(angle)), placed(np.sin(angle))
        mixed.append(np.block([[c, d], [-d, c]]) * np.sqrt(2.0 / points))
    mixed = np.stack(mixed)
    return tuple(
        np.stack([widened(table), widened(np.swapaxes(table, 1, 2))]) for table in (real, mixed)
    )


def geometry(points, bands, rows, width):
    total = rows * bands
    latitude = 0.5 * np.pi - (np.arange(total) + 0.5) * (np.pi / total)
    out = []
    for band in range(bands):
        own = latitude[band * rows : (band + 1) * rows]
        cos_lat, sin_lat = np.repeat(np.cos(own), width), np.repeat(np.sin(own), width)
        stretch = points / (2.0 * total) / cos_lat
        zero, one = np.zeros_like(cos_lat), np.ones_like(cos_lat)
        pairs = (
            (0.5 * stretch, 0.5 * one),
            (0.5 * stretch, zero),
            (0.5 / cos_lat, zero),
            (coriolis_rate * sin_lat, -coriolis_rate * sin_lat),
            (zero, cos_lat),
            (zero, zero),
            (zero, zero),
            (zero, zero),
        )
        out.extend(np.concatenate(pair) for pair in pairs)
    return np.stack(out).astype(np.float32)


def roll(value, shift):
    width = value.shape[-1]
    shift = shift % width
    if shift == 0:
        return value
    if width == 128:
        return pltpu.roll(value, shift, 1)
    return jnp.concatenate([value[:, width - shift :], value[:, : width - shift]], axis=1)


def dot(a, b):
    return jnp.dot(a, b, preferred_element_type=jnp.float32)


def split(value):
    hi = value.astype(jnp.bfloat16)
    return hi, (value - hi.astype(jnp.float32)).astype(jnp.bfloat16)


def kernel(
    dims,
    u_hbm,
    v_hbm,
    h_hbm,
    speed_hbm,
    cutoff_ref,
    geo_hbm,
    real_hbm,
    mixed_hbm,
    u_out,
    v_out,
    h_out,
    u_ref,
    v_ref,
    h_ref,
    speed_ref,
    geo_ref,
    real_t,
    mixed_t,
    send1,
    recv1,
    send2,
    recv2,
    base_uv,
    base_h,
    cur_uv,
    cur_h,
    tend_uv,
    tend_h,
    y_in,
    y_out,
    halo_send,
    halo_recv,
    table_sem,
    send1_sem,
    recv1_sem,
    send2_sem,
    recv2_sem,
    hsend_sem,
    hrecv_sem,
):
    bands, devs, cells, rows, width, pad, wire, half = dims
    points = cells * devs
    part = points // RADIX
    subs = devs // RADIX
    part_pad = subs * pad
    span = rows * width
    slab = 2 * span
    levels = width * devs
    me = lax.axis_index("lon")
    band = lax.axis_index("lat")
    has_north = band > 0
    has_south = band < bands - 1

    local = [
        pltpu.make_async_copy(source, target, table_sem.at[n])
        for n, (source, target) in enumerate(
            (
                (u_hbm, u_ref),
                (v_hbm, v_ref),
                (h_hbm, h_ref),
                (speed_hbm, speed_ref),
                (geo_hbm, geo_ref),
                (real_hbm, real_t),
                (mixed_hbm, mixed_t),
            )
        )
    ]
    for copy in local:
        copy.start()

    barrier = pltpu.get_barrier_semaphore()

    def greet(k, _):
        pl.semaphore_signal(
            barrier, inc=1, device_id={"lon": lax.rem(me + k, devs)}, device_id_type=MESH
        )
        return 0

    lax.fori_loop(1, devs, greet, 0)

    @pl.when(has_north)
    def _():
        pl.semaphore_signal(barrier, inc=1, device_id={"lat": band - 1}, device_id_type=MESH)

    @pl.when(has_south)
    def _():
        pl.semaphore_signal(barrier, inc=1, device_id={"lat": band + 1}, device_id_type=MESH)

    pl.semaphore_wait(
        barrier, devs - 1 + has_north.astype(jnp.int32) + has_south.astype(jnp.int32)
    )

    for copy in local[:3]:
        copy.wait()

    lane_lev = lax.broadcasted_iota(jnp.int32, (cells, levels), 1)
    fields = (u_ref, v_ref, h_ref)
    uv_units = [(fields[n // rows], n % rows, 0) for n in range(2 * rows)]
    h_units = [(h_ref, n % rows, (n // rows) * (cells - half)) for n in range(2 * rows)]

    def packed(units, count, peer):
        total = jnp.zeros((count, levels), jnp.float32)
        lane = lane_lev[:count]
        for n, (ref, row, start) in enumerate(units):
            piece = ref[pl.ds(row + rows * start, count, stride=rows), :]
            shift = lax.rem(n * width - peer * width + levels, levels)
            piece = pltpu.roll(piece, shift, 1)
            total = jnp.where((lane >= n * width) & (lane < (n + 1) * width), piece, total)
        return total[:, :slab]

    def fill(target, slot, peer):
        target[slot, wire - 8 : wire, :] = jnp.zeros((8, slab), jnp.float32)
        target[slot, 0:cells, :] = packed(uv_units, cells, peer)
        target[slot, wire : wire + half, :] = packed(h_units, half, peer)

    def copy1(peer, index):
        return pltpu.make_async_remote_copy(
            src_ref=send1.at[peer],
            dst_ref=recv1.at[index],
            send_sem=send1_sem.at[peer],
            recv_sem=recv1_sem.at[index],
            device_id={"lon": peer},
            device_id_type=MESH,
        )

    def copy2(peer, index):
        return pltpu.make_async_remote_copy(
            src_ref=send2.at[peer],
            dst_ref=recv2.at[index],
            send_sem=send2_sem.at[peer],
            recv_sem=recv2_sem.at[index],
            device_id={"lon": peer},
            device_id_type=MESH,
        )

    def partner(k):
        k = devs - k
        if devs & (devs - 1):
            return lax.rem(me + k, devs)
        peer, bit = 0, 1
        while bit < devs:
            peer = peer + bit * ((me // bit + k // bit) % 2)
            bit *= 2
        return peer

    def out1(k, _):
        peer = partner(k)
        fill(send1, peer, peer)
        copy1(peer, me).start()
        return 0

    lax.fori_loop(1, devs, out1, 0)
    fill(recv1, me, me)

    for copy in local[3:5]:
        copy.wait()
    lane = lax.broadcasted_iota(jnp.int32, (1, slab), 1)
    low = lane < span
    groups = devs // 4
    my_group = me // 4
    all_speeds = jnp.broadcast_to(speed_ref[...], (8, levels))
    own_first = pltpu.roll(all_speeds, lax.rem(levels - me * width, levels), 1)
    lane8 = lax.broadcasted_iota(jnp.int32, (8, levels), 1)
    speed = jnp.zeros((8, levels), jnp.float32)
    cut = jnp.zeros((1, slab), jnp.float32)
    for n in range(2 * rows):
        moved = pltpu.roll(own_first, n * width, 1) if n else own_first
        speed = jnp.where((lane8 >= n * width) & (lane8 < (n + 1) * width), moved, speed)
        row_cut = cutoff_ref[band * rows + n % rows].astype(jnp.float32)
        cut = jnp.where((lane >= n * width) & (lane < (n + 1) * width), row_cut, cut)
    cut = jnp.concatenate([cut, cut], axis=1)
    geo = geo_ref[pl.ds(pl.multiple_of(band * 8, 8), 8), :]
    scaled = geo * speed[:, :slab]
    k1, k2, k3 = scaled[0:1], scaled[1:2], scaled[2:3]
    fcor, cosl = geo[3:4], geo[4:5]

    @pl.when(band == 0)
    def _():
        for t in range(3):
            halo_recv[t, 0] = jnp.zeros(halo_recv.shape[2:], jnp.float32)

    @pl.when(band == bands - 1)
    def _():
        for t in range(3):
            halo_recv[t, 1] = jnp.zeros(halo_recv.shape[2:], jnp.float32)

    def unpack(b):
        uv = recv1[b, 0:wire, :]
        hp = recv1[b, wire : wire + half, :]
        other = roll(hp, span)
        for buf_uv, buf_h, at in ((base_uv, base_h, 0), (cur_uv, cur_h, 8)):
            zeros = jnp.zeros((16, slab), jnp.float32)
            buf_uv[b, at + pad - 16 : at + pad, :] = zeros
            buf_h[b, at + pad - 16 : at + pad, :] = zeros
            if at:
                buf_uv[b, at + pad : at + pad + 8, :] = zeros[:8]
                buf_h[b, at + pad : at + pad + 8, :] = zeros[:8]
            buf_uv[b, at : at + wire, :] = uv
            buf_h[b, at : at + half, :] = hp
            buf_h[b, at + cells - half : at + cells, :] = other

    def halo_copy(t, side, g):
        return pltpu.make_async_remote_copy(
            src_ref=halo_send.at[t, side, g],
            dst_ref=halo_recv.at[t, side, g],
            send_sem=hsend_sem.at[t, side, g],
            recv_sem=hrecv_sem.at[t, side, g],
            device_id={"lat": band + 1 if side == 0 else band - 1},
            device_id_type=MESH,
        )

    def send_halos(t, g):
        south = jnp.zeros((pad, slab), jnp.float32)
        north = jnp.zeros((pad, slab), jnp.float32)
        for j in range(4):
            b = g * 4 + j
            h = cur_h[b, 8 : 8 + pad, :]
            vc = cur_uv[b, 8 : 8 + pad, :] * cosl
            at = 2 * width * j
            on_h = (lane >= at) & (lane < at + width)
            on_v = (lane >= at + width) & (lane < at + 2 * width)
            south = jnp.where(on_h, roll(h, at - (span - width)), south)
            south = jnp.where(on_v, roll(vc, at + width - (slab - width)), south)
            north = jnp.where(on_h, roll(h, at), north)
            north = jnp.where(on_v, roll(vc, at + width - span), north)
        halo_send[t, 0, g] = south
        halo_send[t, 1, g] = north

        @pl.when(has_south)
        def _():
            halo_copy(t, 0, g).start()

        @pl.when(has_north)
        def _():
            halo_copy(t, 1, g).start()

    def in1(k, _):
        g = lax.rem(my_group + k, groups)
        for j in range(4):
            b = g * 4 + j

            @pl.when(b != me)
            def _():
                copy1(b, b).wait_recv()

            unpack(b)
        send_halos(0, g)
        return 0

    lax.fori_loop(0, groups, in1, 0)

    def wrap_rows():
        def one(b, _):
            before = lax.rem(b + devs - 1, devs)
            after = lax.rem(b + 1, devs)
            for buf in (cur_uv, cur_h):
                buf[b, 7:8, :] = buf[before, 7 + cells : 8 + cells, :]
                buf[b, 8 + cells : 9 + cells, :] = buf[after, 8:9, :]
            return 0

        lax.fori_loop(0, devs, one, 0)

    def wait_halos(t, g):
        @pl.when(has_north)
        def _():
            halo_copy(t, 0, g).wait_recv()

        @pl.when(has_south)
        def _():
            halo_copy(t, 1, g).wait_recv()

    chunk = 48 if pad % 48 == 0 else 16

    def tendency(b, top, at, from_north, from_south):
        uv = cur_uv[b, 8 + top : 8 + top + chunk, :]
        h = cur_h[b, 8 + top : 8 + top + chunk, :]
        duv = cur_uv[b, 9 + top : 9 + top + chunk, :] - cur_uv[b, 7 + top : 7 + top + chunk, :]
        dh = cur_h[b, 9 + top : 9 + top + chunk, :] - cur_h[b, 7 + top : 7 + top + chunk, :]
        vc = uv * cosl
        h_n = jnp.where(lane < width, roll(from_north, -at), roll(h, width))
        h_s = jnp.where(
            lane >= span - width, roll(from_south, span - width - at), roll(h, -width)
        )
        v_n = jnp.where(
            lane < span + width, roll(from_north, span - width - at), roll(vc, width)
        )
        v_s = jnp.where(
            lane >= slab - width, roll(from_south, slab - 2 * width - at), roll(vc, -width)
        )
        mh = h_n - h_s
        mv = v_n - v_s
        tend_uv[b, top : top + chunk, :] = fcor * roll(uv, span) - k1 * jnp.where(low, dh, roll(mh, span))
        tend_h[b, top : top + chunk, :] = -(k2 * duv + k3 * roll(mv, span))

    def tendencies(t):
        def group(k, _):
            g = lax.rem(my_group + k, groups)
            wait_halos(t, g)
            for j in range(4):
                b = g * 4 + j
                at = 2 * width * j
                for top in range(0, pad, chunk):
                    tendency(b, top, at, halo_recv[t, 0, g, top : top + chunk, :],
                             halo_recv[t, 1, g, top : top + chunk, :])
            return 0

        lax.fori_loop(0, groups, group, 0)

    def start_of(s):
        return 3 * part_pad * (s if s < 2 else 2 * s - 2)

    def put(s, half_at, j, top, piece, value):
        hi, lo = split(value)
        height = part_pad if s < 2 else 2 * part_pad
        at = start_of(s) + half_at * part_pad + j * pad
        columns = slice(piece * slab, (piece + 1) * slab)
        for n, part_of in enumerate((hi, lo, hi)):
            spot = pl.ds(pl.multiple_of(at + n * height + top, 16), 16)
            y_in[spot, columns] = part_of

    def each_chunk(body):
        def one(n, _):
            body(pl.multiple_of(n * 16, 16))
            return 0

        lax.fori_loop(0, pad // 16, one, 0)

    def forward(top):
        for j in range(subs):
            for piece, buf in enumerate((tend_uv, tend_h)):
                x = [buf[g * subs + j, pl.ds(top, 16), :] for g in range(RADIX)]
                a = [x[n] + x[n + 4] for n in range(4)]
                d = [x[n] - x[n + 4] for n in range(4)]
                plus, minus = a[0] + a[2], a[1] + a[3]
                put(0, 0, j, top, piece, plus + minus)
                put(1, 0, j, top, piece, plus - minus)
                less, more = ROOT * (d[1] - d[3]), ROOT * (d[1] + d[3])
                put(2, 0, j, top, piece, d[0] + less)
                put(2, 1, j, top, piece, -d[2] - more)
                put(3, 0, j, top, piece, a[0] - a[2])
                put(3, 1, j, top, piece, a[3] - a[1])
                put(4, 0, j, top, piece, d[0] - less)
                put(4, 1, j, top, piece, d[2] - more)

    def kept(wave, coefs):
        nearest = jnp.minimum(wave, points - wave).astype(jnp.float32)
        hi, lo = split(jnp.where(nearest <= cut, coefs, 0.0))
        return jnp.concatenate([hi, lo, hi], axis=0)

    def through():
        row = lax.broadcasted_iota(jnp.int32, (part_pad, 2 * slab), 0)
        mid = part // 2
        even = RADIX * jnp.where(row <= mid, row, row - mid)
        odd = RADIX * jnp.where(row < mid, row, row - mid) + RADIX // 2
        for s, wave in enumerate((even, odd)):
            at = pl.ds(s * part_pad, part_pad)
            coefs = dot(real_t[0, s], y_in[pl.ds(start_of(s), 3 * part_pad), :])
            y_out[at, :] = dot(real_t[1, s], kept(wave, coefs))
        both = lax.broadcasted_iota(jnp.int32, (2 * part_pad, 2 * slab), 0)
        wave8 = RADIX * jnp.where(both < part_pad, both, both - part_pad)

        for s in range(3):
            at = pl.ds((2 + 2 * s) * part_pad, 2 * part_pad)
            coefs = dot(mixed_t[0, s], y_in[pl.ds(start_of(s + 2), 6 * part_pad), :])
            y_out[at, :] = dot(mixed_t[1, s], kept(wave8 + (s + 1), coefs))

    def backward(top):
        for j in range(subs):
            for piece, buf in enumerate((tend_uv, tend_h)):
                y = [
                    y_out[pl.ds(pl.multiple_of(n * part_pad + j * pad + top, 16), 16), piece * slab : (piece + 1) * slab]
                    for n in range(RADIX)
                ]
                plus, minus = y[0] + y[1], y[0] - y[1]
                e, f = y[2] + y[6], y[7] - y[3]
                buf[0 * subs + j, pl.ds(top, 16), :] = plus + y[4] + e
                buf[4 * subs + j, pl.ds(top, 16), :] = plus + y[4] - e
                buf[2 * subs + j, pl.ds(top, 16), :] = plus - y[4] + f
                buf[6 * subs + j, pl.ds(top, 16), :] = plus - y[4] - f
                m, n = ROOT * (y[2] - y[6]), ROOT * (y[3] + y[7])
                buf[1 * subs + j, pl.ds(top, 16), :] = minus - y[5] + (m - n)
                buf[5 * subs + j, pl.ds(top, 16), :] = minus - y[5] - (m - n)
                buf[3 * subs + j, pl.ds(top, 16), :] = minus + y[5] - (m + n)
                buf[7 * subs + j, pl.ds(top, 16), :] = minus + y[5] + (m + n)

    quarter = rows * bands // 4
    filters = (band * rows < quarter) | (band * rows + rows > rows * bands - quarter)

    for t, (own, new) in enumerate(((0.0, 1.0), (0.75, 0.25), (1.0 / 3.0, 2.0 / 3.0))):
        wrap_rows()
        if t == 0:
            for copy in local[5:]:
                copy.wait()
        tendencies(t)

        @pl.when(filters)
        def _():
            each_chunk(forward)
            through()
            each_chunk(backward)

        def update(k, _):
            g = lax.rem(my_group + k, groups)
            for j in range(4):
                b = g * 4 + j
                for base, cur, tend in ((base_uv, cur_uv, tend_uv), (base_h, cur_h, tend_h)):
                    value = cur[b, 8 : 8 + pad, :] + tend[b]
                    if t > 0:
                        value = own * base[b] + new * value
                    cur[b, 8 : 8 + pad, :] = value
            send_halos(t + 1, g)
            return 0

        if t < 2:
            lax.fori_loop(0, groups, update, 0)

    def result(target, slot, b):
        def final(base, cur, tend, start, count):
            value = cur[b, 8 + start : 8 + start + count, :] + tend[b, start : start + count, :]
            return own * base[b, start : start + count, :] + new * value

        target[slot, 0:wire, :] = final(base_uv, cur_uv, tend_uv, 0, wire)
        h_first = final(base_h, cur_h, tend_h, 0, half)
        h_last = final(base_h, cur_h, tend_h, cells - half, half)
        target[slot, wire : wire + half, :] = jnp.where(low, h_first, roll(h_last, span))

    def out2(k, _):
        peer = partner(k)
        result(send2, peer, peer)
        copy2(peer, me).start()
        return 0

    lax.fori_loop(1, devs, out2, 0)
    result(recv2, me, me)

    def in2(k, _):
        peer = lax.rem(me + devs - k, devs)
        copy2(peer, peer).wait_recv()
        return 0

    lax.fori_loop(1, devs, in2, 0)

    def wide(value):
        if slab == levels:
            return value
        fill_up = jnp.zeros((value.shape[0], levels - slab), jnp.float32)
        return jnp.concatenate([value, fill_up], axis=1)

    outs = (u_out, v_out, h_out)

    def gathered(n, first, count):
        total = jnp.zeros((count, levels), jnp.float32)
        here = lane_lev[:count]
        for d in range(devs):
            piece = wide(recv2[d, first : first + count, :])
            piece = pltpu.roll(piece, (d - n) * width % levels, 1)
            total = jnp.where((here >= d * width) & (here < (d + 1) * width), piece, total)
        return total

    for n in range(2 * rows):
        ref = outs[n // rows]
        ref[pl.ds(n % rows, cells, stride=rows), :] = gathered(n, 0, cells)
        start = (n // rows) * (cells - half)
        h_out[pl.ds(n % rows + rows * start, half, stride=rows), :] = gathered(n, wire, half)

    def done(k, _):
        peer = lax.rem(me + k, devs)
        copy1(peer, me).wait_send()
        copy2(peer, me).wait_send()
        return 0

    lax.fori_loop(1, devs, done, 0)

    for t in range(3):
        for g in range(groups):
            @pl.when(has_south)
            def _():
                halo_copy(t, 0, g).wait_send()

            @pl.when(has_north)
            def _():
                halo_copy(t, 1, g).wait_send()


def shards(geo_tab, real_tab, mixed_tab, bands, devs, pad, u_wind, v_wind, height, wave_speed, cutoff):
    cells, rows, levels = u_wind.shape
    width = levels // devs
    slab = 2 * rows * width
    wire = round_up(cells, 8)
    half = round_up(-(-cells // 2), 8)
    f32, bf16 = jnp.float32, jnp.bfloat16
    part_pad = devs // RADIX * pad
    dims = (bands, devs, cells, rows, width, pad, wire, half)
    vmem = pl.BlockSpec(memory_space=pltpu.VMEM)
    anywhere = pl.BlockSpec(memory_space=pltpu.HBM)
    flat = jax.ShapeDtypeStruct((cells * rows, levels), f32)
    dma = pltpu.SemaphoreType.DMA
    outs = pl.pallas_call(
        functools.partial(kernel, dims),
        out_shape=(flat, flat, flat),
        in_specs=[anywhere] * 4 + [pl.BlockSpec(memory_space=pltpu.SMEM)] + [anywhere] * 3,
        out_specs=(vmem, vmem, vmem),
        scratch_shapes=[
            pltpu.VMEM(flat.shape, f32),
            pltpu.VMEM(flat.shape, f32),
            pltpu.VMEM(flat.shape, f32),
            pltpu.VMEM((1, levels), f32),
            pltpu.VMEM(geo_tab.shape, f32),
            pltpu.VMEM(real_tab.shape, bf16),
            pltpu.VMEM(mixed_tab.shape, bf16),
            pltpu.VMEM((devs, wire + half, slab), f32),
            pltpu.VMEM((devs, wire + half, slab), f32),
            pltpu.VMEM((devs, wire + half, slab), f32),
            pltpu.VMEM((devs, wire + half, slab), f32),
            pltpu.VMEM((devs, pad, slab), f32),
            pltpu.VMEM((devs, pad, slab), f32),
            pltpu.VMEM((devs, pad + 16, slab), f32),
            pltpu.VMEM((devs, pad + 16, slab), f32),
            pltpu.VMEM((devs, pad, slab), f32),
            pltpu.VMEM((devs, pad, slab), f32),
            pltpu.VMEM((3 * RADIX * part_pad, 2 * slab), bf16),
            pltpu.VMEM((RADIX * part_pad, 2 * slab), f32),
            pltpu.VMEM((3, 2, devs // 4, pad, slab), f32),
            pltpu.VMEM((3, 2, devs // 4, pad, slab), f32),
            dma((7,)),
            dma((devs,)),
            dma((devs,)),
            dma((devs,)),
            dma((devs,)),
            dma((3, 2, devs // 4)),
            dma((3, 2, devs // 4)),
        ],
        compiler_params=pltpu.CompilerParams(
            collective_id=0, has_side_effects=True, vmem_limit_bytes=48 * 1024 * 1024
        ),
    )(
        u_wind.reshape(cells * rows, levels),
        v_wind.reshape(cells * rows, levels),
        height.reshape(cells * rows, levels),
        wave_speed.reshape(1, levels),
        cutoff,
        jnp.asarray(geo_tab),
        jnp.asarray(real_tab),
        jnp.asarray(mixed_tab),
    )
    return tuple(out.reshape(cells, rows, levels) for out in outs)


def solution(mesh):
    bands, devs = mesh.shape["lat"], mesh.shape["lon"]

    def step(u_wind, v_wind, height, wave_speed, cutoff):
        points = u_wind.shape[0]
        pad = round_up(points // devs + 1, 16)
        real_tab, mixed_tab = tables(points, points // devs, pad)
        rows, width = u_wind.shape[1] // bands, u_wind.shape[2] // devs
        geo_tab = geometry(points, bands, rows, width)
        spec = P("lon", "lat", None)
        local = functools.partial(shards, geo_tab, real_tab, mixed_tab, bands, devs, pad)
        return jax.shard_map(
            local,
            mesh=mesh,
            in_specs=(spec, spec, spec, P(), P()),
            out_specs=(spec, spec, spec),
            check_vma=False,
        )(u_wind, v_wind, height, wave_speed, cutoff)

    return step
```
